32 devices in a mesh: row: 4 (over z), col: 8 (over y, x, core).
Axes of the slice: x: 2, y: 2, z: 4, core: 2. Of those that a mesh axis runs over, the one named last changes fastest.
Arguments:
- positions: float32 [1024, 24576], P('row', 'col'), may hold values from -2.5 to 2.5
- momenta: float32 [1024, 24576], P('row', 'col'), may hold values from -2.5 to 2.5
- couplings: float32 [24576, 24576], P('row', 'col'), may hold values from -0.0390625 to 0.0390625
Outputs:
- positions_next: float32 [1024, 24576], P('row', 'col')
- momenta_next: float32 [1024, 24576], P('row', 'col')
The draws below stay inside these ranges and needn't reach their ends.
All inputs are finite; a program needn't handle non-finite values.
Results may differ from the reference program's by a relative error of at most 0.00005.
Values sent between devices are 32-bit elements; how exact they have to be, the bound alone decides.
No kernel may reach another device: no remote copies, remote signals or barrier semaphores. Data moves between devices by JAX's collectives and lax.ppermute only.
A program may use at most 192 MiB of HBM per device.

```python
import jax
import jax.numpy as jnp
from jax import lax

N = 24576
R = 1024


def block_levels(own_key, extent, pieces, smallest, largest):
    def one(position, blocks):
        draws = jax.random.uniform(jax.random.fold_in(jax.random.fold_in(own_key, 6), position), (blocks,), jnp.float32, smallest / len(pieces), largest / len(pieces))
        return jnp.repeat(jnp.exp(draws), extent[position] // blocks).reshape((-1,) + (1,) * (len(extent) - position - 1))

    factor_of = one(*pieces[0])
    for cut in pieces[1:]:
        factor_of = factor_of * one(*cut)
    return factor_of


def normal_values(own_key, extent, deviation, bound, pieces=(), kind=jnp.bfloat16):
    array = deviation * jax.random.normal(own_key, extent, jnp.float32)
    if pieces:
        array = array * block_levels(own_key, extent, pieces, -0.22, 0.18)
    return jnp.clip(array, -bound, bound).astype(kind)


def setup_inputs(seed: int = 0) -> dict:
    arg_keys = jax.random.split(jax.random.key(seed), 4)
    positions = normal_values(arg_keys[0], (R, N), 0.4, 2.5, ((0, 4), (1, 8)), jnp.float32)
    momenta = normal_values(arg_keys[1], (R, N), 0.4, 2.5, ((0, 4), (1, 8)), jnp.float32)
    couplings = normal_values(arg_keys[2], (N, N), N ** -0.5, 0.0390625, ((0, 4), (1, 8)), jnp.float32)
    return dict(positions=positions, momenta=momenta, couplings=couplings)


time_step = 0.5
kerr_rate = 1.0
pump_rate = 0.6
detuning = 0.4
coupling_gain = 1.5


def reference(positions, momenta, couplings):
    coupled = jnp.dot(positions, couplings, precision=lax.Precision.HIGHEST, preferred_element_type=jnp.float32)
    radius = positions * positions + momenta * momenta
    momenta_next = momenta + time_step * (-(kerr_rate * radius - pump_rate + detuning) * positions + coupling_gain * coupled)
    radius_next = positions * positions + momenta_next * momenta_next
    positions_next = positions + time_step * (kerr_rate * radius_next + pump_rate + detuning) * momenta_next
    return positions_next, momenta_next
```

```python
import functools

import jax
import jax.numpy as jnp
from jax import lax
from jax.experimental import pallas as pl
from jax.experimental.pallas import tpu as pltpu
from jax.sharding import PartitionSpec as P

time_step = 0.5
kerr_rate = 1.0
pump_rate = 0.6
detuning = 0.4
coupling_gain = 1.5

CHUNKS = 3
VMEM = 56 * 2**20
f32, bf16 = jnp.float32, jnp.bfloat16


def halves(x):
    high = x.astype(bf16)
    return high, (x - high.astype(f32)).astype(bf16)


def products(split_ref, c_ref, o_ref, depth):
    k = pl.program_id(1)
    columns = pl.ds(pl.multiple_of(k * depth, depth), depth)
    high, low = halves(c_ref[...])
    p_high = split_ref[0, :, columns]
    part = jnp.dot(p_high, high, preferred_element_type=f32)
    part += jnp.dot(split_ref[1, :, columns], high, preferred_element_type=f32)
    part += jnp.dot(p_high, low, preferred_element_type=f32)

    @pl.when(k == 0)
    def _():
        o_ref[...] = part

    @pl.when(k > 0)
    def _():
        o_ref[...] += part


def first_kernel(p_ref, c_ref, o_ref, split_ref):
    sites, _, rows, depth = p_ref.shape
    k = pl.program_id(1)

    @pl.when(pl.program_id(0) == 0)
    def _():
        columns = pl.ds(pl.multiple_of(k * depth, depth), depth)
        for j in range(sites):
            high, low = halves(p_ref[j, k])
            split_ref[0, pl.ds(j * rows, rows), columns] = high
            split_ref[1, pl.ds(j * rows, rows), columns] = low

    products(split_ref, c_ref, o_ref, depth)


def next_kernel(split_ref, c_ref, o_ref):
    products(split_ref, c_ref, o_ref, c_ref.shape[0])


def block_product(block, couplings, parts, start, width):
    depth = couplings.shape[0] // parts
    first = block.ndim == 4
    rows = block.shape[0] * block.shape[2] if first else block.shape[1]
    split = jax.ShapeDtypeStruct((2, rows, depth * parts), bf16)
    tile = min(512, width)
    whole = pl.BlockSpec(block.shape, lambda i, k: (0,) * block.ndim, pipeline_mode=pl.Buffered(1))
    out_shape = [jax.ShapeDtypeStruct((rows, width), f32)]
    out_specs = [pl.BlockSpec((rows, tile), lambda i, k: (0, i))]
    if first:
        out_shape.append(split)
        out_specs.append(pl.BlockSpec(split.shape, lambda i, k: (0, 0, 0)))
    out = pl.pallas_call(
        first_kernel if first else next_kernel,
        grid=(width // tile, parts),
        in_specs=[whole, pl.BlockSpec((depth, tile), lambda i, k: (k, start // tile + i))],
        out_specs=out_specs,
        out_shape=out_shape,
        compiler_params=pltpu.CompilerParams(vmem_limit_bytes=VMEM),
        cost_estimate=pl.CostEstimate(flops=0, bytes_accessed=2**20, transcendentals=0),
    )(block, couplings)
    return out[0], (out[1] if first else block)


def after(x, *others):
    return lax.optimization_barrier((x, *others))[0]


class Plan:
    def __init__(self, n, cols):
        self.n, self.cols, self.ratio = n, cols, cols // n
        assert self.ratio * n == cols
        self.order = [[self.shift(z, a) for a in range(n - 1, -1, -1)] for z in range(n)]
        self.slot = [[self.order[z].index(s) for s in range(n)] for z in range(n)]

    def shift(self, a, b):
        return a ^ b if self.n & (self.n - 1) == 0 else (a + b) % self.n

    def unshift(self, a, b):
        return a ^ b if self.n & (self.n - 1) == 0 else (a - b) % self.n

    def site_pairs(self, m):
        r = self.ratio
        return [(q * r + c, self.shift(q, m) * r + c) for q in range(self.n) for c in range(r)]


def shift(plan, a, b):
    return a ^ b if plan.n & (plan.n - 1) == 0 else lax.rem(a + b, plan.n)


def unshift(plan, a, b):
    return a ^ b if plan.n & (plan.n - 1) == 0 else lax.rem(a - b + plan.n, plan.n)


def one_of(values, index):
    out = values[0]
    for i in range(1, len(values)):
        out = jnp.where(index == i, values[i], out)
    return out


def pick(values, choice, index):
    used = sorted({c for c in choice if c is not None})
    out = values[used[0]]
    for c in used[1:]:
        mine = functools.reduce(jnp.logical_or, [index == i for i, v in enumerate(choice) if v == c])
        out = jnp.where(mine, values[c], out)
    return out


def spread_sites(plan, positions, col):
    n = plan.n
    site = col // plan.ratio
    rows = positions.shape[0] // n
    arrived = []
    for m in range(n):
        j = shift(plan, site, m)
        part = lax.dynamic_slice_in_dim(positions, j * rows, rows, axis=0)
        arrived.append(part if m == 0 else lax.ppermute(part, "col", plan.site_pairs(m)))
    return [one_of(arrived, unshift(plan, site, q)) for q in range(n)]


def gather_slot(plan, k, spread, row):
    n = plan.n
    target = [[plan.order[z][k] for z in range(n)].index(r) for r in range(n)]
    part = pick(spread, target, row)
    pairs = [(r, target[r]) for r in range(n)]
    if any(a != b for a, b in pairs):
        part = lax.ppermute(part, "row", pairs)
    whole = lax.all_gather(part, "col", axis=0, tiled=False)
    return whole.reshape(n, plan.ratio, *part.shape)


def per_device(plan, positions, momenta, couplings):
    n = plan.n
    row, col = lax.axis_index("row"), lax.axis_index("col")
    width = positions.shape[1]
    chunk = width // CHUNKS
    lanes = [slice(c * chunk, (c + 1) * chunk) for c in range(CHUNKS)]

    spread = spread_sites(plan, positions, col)
    gathered = [gather_slot(plan, k, spread, row) for k in range(n)]

    partial = [[None] * CHUNKS for _ in range(n)]
    from_below, from_above = [None] * CHUNKS, [None] * CHUNKS
    last = None
    for k in range(n):
        block = gathered[k]
        for c in range(CHUNKS):
            if last is not None:
                block = after(block, last)
            last, block = block_product(block, couplings, plan.ratio, lanes[c].start, chunk)
            partial[k][c] = last
            t = k
            if t == n - 1:
                continue
            up = [plan.slot[z][n - 1 - t + z] if z <= t else None for z in range(n)]
            down = [plan.slot[z][z - (n - 1 - t)] if z >= n - 1 - t else None for z in range(n)]
            here = [partial[i][c] for i in range(n)]
            above, below = pick(here, up, row), pick(here, down, row)
            if t:
                above, below = above + from_below[c], below + from_above[c]
            from_below[c] = lax.ppermute(above, "row", [(z, z + 1) for z in range(t + 1)])
            from_above[c] = lax.ppermute(below, "row", [(z, z - 1) for z in range(n - 1 - t, n)])

    outs = []
    for c in range(CHUNKS):
        coupled = pick([partial[k][c] for k in range(n)], [plan.slot[z][z] for z in range(n)], row)
        if n > 1:
            coupled = coupled + from_below[c] + from_above[c]
        x, y = positions[:, lanes[c]], momenta[:, lanes[c]]
        radius = x * x + y * y
        y_next = y + time_step * (
            -(kerr_rate * radius - pump_rate + detuning) * x + coupling_gain * coupled
        )
        radius_next = x * x + y_next * y_next
        x_next = x + time_step * (kerr_rate * radius_next + pump_rate + detuning) * y_next
        outs.append((x_next, y_next))
    return (
        jnp.concatenate([o[0] for o in outs], axis=1),
        jnp.concatenate([o[1] for o in outs], axis=1),
    )


def solution(mesh):
    placed = (P("row", "col"), P("row", "col"), P("row", "col"))
    plan = Plan(mesh.shape["row"], mesh.shape["col"])

    def step(positions, momenta, couplings):
        return per_device(plan, positions, momenta, couplings)

    return jax.shard_map(
        step,
        mesh=mesh,
        in_specs=placed,
        out_specs=(P("row", "col"), P("row", "col")),
        check_vma=False,
    )
```

```python
import functools

import jax
import jax.numpy as jnp
from jax import lax
from jax.experimental import pallas as pl
from jax.experimental.pallas import tpu as pltpu
from jax.sharding import PartitionSpec as P

time_step = 0.5
kerr_rate = 1.0
pump_rate = 0.6
detuning = 0.4
coupling_gain = 1.5

CHUNKS = 2
SHARES = 2
WORK = 1
VMEM = 56 * 2**20
f32, bf16 = jnp.float32, jnp.bfloat16


def halves(x):
    high = x.astype(bf16)
    return high, (x - high.astype(f32)).astype(bf16)


def products(split_ref, c_ref, add_ref, o_ref, share):
    k, (h, of), depth = pl.program_id(1), share, c_ref.shape[0]
    columns = pl.ds(pl.multiple_of((k * of + h) * depth, depth), depth)
    high, low = halves(c_ref[...])
    p_high = split_ref[0, :, columns]
    part = jnp.dot(p_high, high, preferred_element_type=f32)
    part += jnp.dot(split_ref[1, :, columns], high, preferred_element_type=f32)
    part += jnp.dot(p_high, low, preferred_element_type=f32)

    @pl.when(k == 0)
    def _():
        o_ref[...] = part if add_ref is None else add_ref[...] + part

    @pl.when(k > 0)
    def _():
        o_ref[...] += part


def put(split_ref, piece, row, column):
    rows, columns = pl.ds(row, piece.shape[0]), pl.ds(column, piece.shape[1])
    split_ref[0, rows, columns], split_ref[1, rows, columns] = halves(piece)


def opening_kernel(parts, share, more, *refs):
    offsets, pieces, (c_ref, *refs) = refs[0], refs[1 : -3 - 2 * more], refs[-3 - 2 * more :]
    o_ref, split_ref = refs[-2:]
    sites = len(pieces) // parts

    @pl.when((pl.program_id(0) == 0) & (pl.program_id(1) == 0))
    def _():
        if more:
            split_ref[...] = refs[1][...]
        for m in range(sites):
            for d in range(parts):
                piece = pieces[m * parts + d][...]
                row = pl.multiple_of(offsets[m], piece.shape[0])
                column = pl.multiple_of(offsets[sites + d], piece.shape[1])
                put(split_ref, piece, row, column)

    products(split_ref, c_ref, refs[0] if more else None, o_ref, share)


def split_kernel(added, split_ref, c_ref, *refs):
    products(split_ref, c_ref, refs[0] if added else None, refs[-1], (0, 1))


def whole_kernel(added, block_ref, c_ref, *refs):
    o_ref, split_ref = refs[-2:]
    k, depth = pl.program_id(1), c_ref.shape[0]

    @pl.when(pl.program_id(0) == 0)
    def _():
        for j in range(block_ref.shape[0]):
            put(split_ref, block_ref[j, k], j * block_ref.shape[2], pl.multiple_of(k * depth, depth))

    products(split_ref, c_ref, refs[0] if added else None, o_ref, (0, 1))


def step_kernel(terms, x_ref, y_ref, *refs):
    coupled = refs[0][...]
    for term in refs[1:terms]:
        coupled += term[...]
    x, y = x_ref[...], y_ref[...]
    radius = x * x + y * y
    y_next = y + time_step * (-(kerr_rate * radius - pump_rate + detuning) * x + coupling_gain * coupled)
    radius_next = x * x + y_next * y_next
    refs[-2][...] = x + time_step * (kerr_rate * radius_next + pump_rate + detuning) * y_next
    refs[-1][...] = y_next


def oscillate(terms, positions, momenta, lanes, outs):
    rows, width = positions.shape[0], lanes.stop - lanes.start
    tile = tile_of(width)
    there = pl.BlockSpec((rows, tile), lambda i: (0, lanes.start // tile + i))
    here = pl.BlockSpec((rows, tile), lambda i: (0, i))
    first = 2 + len(terms)
    return pl.pallas_call(
        functools.partial(step_kernel, len(terms)),
        grid=(width // tile,),
        in_specs=[there, there] + [here] * len(terms) + [pl.BlockSpec(memory_space=pl.ANY)] * len(outs),
        out_specs=[there, there],
        out_shape=[jax.ShapeDtypeStruct(positions.shape, f32)] * 2,
        input_output_aliases={first + i: i for i in range(len(outs))},
        name="oscillate",
    )(positions, momenta, *terms, *outs)


def tile_of(width):
    return max(t for t in range(128, 513, 128) if width % t == 0)


def call(kernel, operands, couplings, lanes, parts, rows, share=(0, 1), add=(), offsets=None, keep=False):
    h, of = share
    start, width = lanes.start, lanes.stop - lanes.start
    depth = couplings.shape[0] // (parts * of)
    tile = tile_of(width)

    def whole(x):
        return pl.BlockSpec(x.shape, lambda i, k, *_: (0,) * len(x.shape), pipeline_mode=pl.Buffered(1))

    result = pl.BlockSpec((rows, tile), lambda i, k, *_: (0, i))
    couple = pl.BlockSpec((depth, tile), lambda i, k, *_: (k * of + h, start // tile + i))
    in_specs, values = [whole(x) for x in operands] + [couple], [*operands, couplings]
    in_specs += [result if i == 0 else whole(x) for i, x in enumerate(add)]
    values += add
    out_shape, out_specs = [jax.ShapeDtypeStruct((rows, width), f32)], [result]
    split = jax.ShapeDtypeStruct((2, rows, couplings.shape[0]), bf16)
    if keep:
        out_shape.append(split)
        out_specs.append(pl.BlockSpec(split.shape, lambda i, k, *_: (0, 0, 0)))
    out = pl.pallas_call(
        kernel,
        grid_spec=pltpu.PrefetchScalarGridSpec(
            num_scalar_prefetch=int(offsets is not None),
            grid=(width // tile, parts),
            in_specs=in_specs,
            out_specs=out_specs,
        ),
        out_shape=out_shape,
        compiler_params=pltpu.CompilerParams(vmem_limit_bytes=VMEM),
        cost_estimate=pl.CostEstimate(flops=WORK * rows * width * depth * parts, bytes_accessed=0, transcendentals=0),
        name="products",
    )(*(() if offsets is None else (offsets,)), *values)
    return out if keep else out[0]


def after(x, *others):
    return lax.optimization_barrier((x, *others))[0]


class Plan:
    def __init__(self, n, cols):
        self.n, self.cols, self.ratio = n, cols, cols // n
        assert self.ratio * n == cols
        self.order = [[self.shift(z, a) for a in range(n - 1, -1, -1)] for z in range(n)]
        self.slot = [[self.order[z].index(s) for s in range(n)] for z in range(n)]

    def shift(self, a, b):
        return a ^ b if self.n & (self.n - 1) == 0 else (a + b) % self.n

    def unshift(self, a, b):
        return a ^ b if self.n & (self.n - 1) == 0 else (a - b) % self.n

    def messages(self, t, k):
        n, rounds = self.n, []
        for z in range(t + 1):
            if z < n - 1 and self.slot[z][n - 1 - t + z] == k:
                pair = [(z, z + 1), (n - 1 - z, n - 2 - z)]
                for others in rounds:
                    both = others + pair
                    if len({a for a, _ in both}) == len({b for _, b in both}) == len(both):
                        others += pair
                        break
                else:
                    rounds.append(pair)
        return rounds

    def sources(self, t, k):
        n, out = self.n, {}
        for pairs in self.messages(t, k):
            out.update((a, 2 * a - b if 0 <= 2 * a - b < n else None) for a, b in pairs)
        if k == t:
            for later in range(t + 1, n - 1):
                for pairs in self.messages(later, k):
                    out.update((a, None) for a, _ in pairs)
        return out

    def site_pairs(self, m):
        r = self.ratio
        return [(q * r + c, self.shift(q, m) * r + c) for q in range(self.n) for c in range(r)]


def shift(plan, a, b):
    return a ^ b if plan.n & (plan.n - 1) == 0 else lax.rem(a + b, plan.n)


def unshift(plan, a, b):
    return a ^ b if plan.n & (plan.n - 1) == 0 else lax.rem(a - b + plan.n, plan.n)


def one_of(values, index):
    out = values[0]
    for i in range(1, len(values)):
        out = jnp.where(index == i, values[i], out)
    return out


def pick(values, choice, index):
    used = sorted({c for c in choice if c is not None})
    out = values[used[0]]
    for c in used[1:]:
        mine = functools.reduce(jnp.logical_or, [index == i for i, v in enumerate(choice) if v == c])
        out = jnp.where(mine, values[c], out)
    return out


def spread_sites(plan, positions, col, start, depth):
    n = plan.n
    site = col // plan.ratio
    rows = positions.shape[0] // n
    arrived = []
    for m in range(n):
        part = lax.dynamic_slice(positions, (shift(plan, site, m) * rows, start), (rows, depth))
        arrived.append(part if m == 0 else lax.ppermute(part, "col", plan.site_pairs(m)))
    return arrived


def exchange_rows(plan, k, arrived, row, col, *before):
    n = plan.n
    target = [[plan.order[z][k] for z in range(n)].index(r) for r in range(n)]
    part = one_of(arrived, unshift(plan, col // plan.ratio, one_of(target, row)))
    if before:
        part = after(part, *before)
    pairs = [(r, target[r]) for r in range(n)]
    return lax.ppermute(part, "row", pairs) if any(a != b for a, b in pairs) else part


def gather_plane(plan, part):
    whole = lax.all_gather(part, "col", axis=0, tiled=False)
    return whole.reshape(plan.n, plan.ratio, *part.shape)


def gather_sites(plan, part):
    return [part if m == 0 else lax.ppermute(part, "col", plan.site_pairs(m)) for m in range(plan.n)]


def gather_parts(plan, pieces):
    r = plan.ratio
    turns = [[(q * r + c, q * r + (c + d) % r) for q in range(plan.n) for c in range(r)] for d in range(r)]
    return [p if d == 0 else lax.ppermute(p, "col", turns[d]) for p in pieces for d in range(r)]


def piece_offsets(plan, rows, depth, start, col):
    n, r = plan.n, plan.ratio
    site, part = col // r, lax.rem(col, r)
    starts = [unshift(plan, site, m) * rows for m in range(n)]
    starts += [lax.rem(part - d + r, r) * depth + start for d in range(r)]
    return jnp.stack(starts).astype(jnp.int32)


class Sums:
    def __init__(self):
        self.arrays = []

    def add(self, array, pairs):
        self.arrays.append((array, {b: a for a, b in pairs}))

    def carried(self, wanted, row):
        def serves(heard, z):
            return heard.get(z) == wanted[z]

        for array, heard in self.arrays:
            if all(serves(heard, z) for z in wanted):
                return array
        out = None
        for array, heard in self.arrays:
            mine = functools.reduce(
                jnp.logical_or, [row == z for z in wanted if wanted[z] is not None and serves(heard, z)], False
            )
            kept = jnp.where(mine, array, 0.0)
            out = kept if out is None else out + kept
        return out


def per_device(plan, positions, momenta, couplings):
    n = plan.n
    row, col = lax.axis_index("row"), lax.axis_index("col")
    width = positions.shape[1]
    chunk = width // CHUNKS
    lanes = [slice(c * chunk, (c + 1) * chunk) for c in range(CHUNKS)]

    depth = width // SHARES
    spread = [spread_sites(plan, positions, col, h * depth, depth) for h in range(SHARES)]
    own = []
    for h in range(SHARES):
        own.append(exchange_rows(plan, 0, spread[h], row, col, *own[-1:]))
    opening = [gather_sites(plan, part) for part in own]
    spread = [jnp.concatenate(share, axis=1) for share in zip(*spread)]
    for k in range(1, n):
        own.append(exchange_rows(plan, k, spread, row, col, *own[SHARES - 1 :][: 1 if k < n - 1 else None]))
    own = own[SHARES - 1 :]

    partial = [[None] * CHUNKS for _ in range(n)]
    sums = [[Sums() for _ in range(CHUNKS)] for _ in range(n)]
    rows, so_far, outs = positions.shape[0], None, []
    for h in range(SHARES):
        pieces = opening[h]
        if h:
            couplings = after(couplings, so_far[0], own[SHARES])
            pieces = [after(piece, so_far[0]) for piece in pieces]
        pieces = gather_parts(plan, pieces)
        so_far = call(
            functools.partial(opening_kernel, plan.ratio, (h, SHARES), so_far is not None),
            pieces,
            couplings,
            lanes[0],
            plan.ratio,
            rows,
            share=(h, SHARES),
            add=so_far or (),
            offsets=piece_offsets(plan, rows // n, width, h * depth, col),
            keep=True,
        )
    partial[0][0], block = so_far
    own = [after(part, partial[0][0], own[-2]) for part in own]
    gathered = [None] + [gather_plane(plan, part) for part in own[1:]]
    couplings = after(couplings, *own[1:])
    last = partial[0][0]
    for t in range(n):
        for c, span in enumerate(lanes):
            add = []
            if 0 < t < n - 1:
                add = [sums[t - 1][c].carried(plan.sources(t, t), row)]
            if t or c:
                before = [array for array, _ in sums[t - 1][c].arrays] if 0 < t < n - 1 else []
                couplings = after(couplings, last, *before)
                first = c == 0 and t > 0
                operand = gathered[t] if first else block
                kernel = functools.partial(whole_kernel if first else split_kernel, len(add))
                out = call(kernel, [operand], couplings, span, plan.ratio, rows, add=add, keep=first)
                last, block = out if first else (out, block)
                partial[t][c] = last
            for k in range(t + 1):
                mine = partial[t][c]
                if k < t:
                    if not plan.messages(t, k):
                        continue
                    mine = after(partial[k][c], partial[t][c]) + sums[t - 1][c].carried(plan.sources(t, k), row)
                for pairs in plan.messages(t, k):
                    sums[t][c].add(lax.ppermute(mine, "row", pairs), pairs)
            if t == n - 1:
                terms = [last] + [array for array, _ in sums[n - 2][c].arrays]
                outs = oscillate(terms, positions, momenta, span, outs)
                couplings = after(couplings, outs[0])
    return outs


def solution(mesh):
    placed = (P("row", "col"), P("row", "col"), P("row", "col"))
    plan = Plan(mesh.shape["row"], mesh.shape["col"])

    def step(positions, momenta, couplings):
        return per_device(plan, positions, momenta, couplings)

    return jax.shard_map(
        step,
        mesh=mesh,
        in_specs=placed,
        out_specs=(P("row", "col"), P("row", "col")),
        check_vma=False,
    )
```

```python
import functools

import jax
import jax.numpy as jnp
from jax import lax
from jax.experimental import pallas as pl
from jax.experimental.pallas import tpu as pltpu
from jax.sharding import PartitionSpec as P

time_step = 0.5
kerr_rate = 1.0
pump_rate = 0.6
detuning = 0.4
coupling_gain = 1.5

CHUNKS = 2
SHARES = 2
WORK = 0
VMEM = 60 * 2**20
f32, bf16 = jnp.float32, jnp.bfloat16


def halves(x):
    high = x.astype(bf16)
    return high, (x - high.astype(f32)).astype(bf16)


def products(split_ref, c_ref, add_ref, o_ref, share):
    k, (h, of), depth = pl.program_id(1), share, c_ref.shape[0]
    columns = pl.ds(pl.multiple_of((k * of + h) * depth, depth), depth)
    high, low = halves(c_ref[...])
    p_high = split_ref[0, :, columns]
    part = jnp.dot(p_high, high, preferred_element_type=f32)
    part += jnp.dot(split_ref[1, :, columns], high, preferred_element_type=f32)
    part += jnp.dot(p_high, low, preferred_element_type=f32)

    @pl.when(k == 0)
    def _():
        o_ref[...] = part if add_ref is None else add_ref[...] + part

    @pl.when(k > 0)
    def _():
        o_ref[...] += part


def put(split_ref, piece, row, column):
    rows, columns = pl.ds(row, piece.shape[0]), pl.ds(column, piece.shape[1])
    split_ref[0, rows, columns], split_ref[1, rows, columns] = halves(piece)


def pieces_kernel(sites, parts, share, added, offsets, *refs):
    (c_ref, *add), (o_ref, split_ref) = refs[-3 - added : -2], refs[-2:]
    pieces = refs[: -3 - added]

    @pl.when((pl.program_id(0) == 0) & (pl.program_id(1) == 0))
    def _():
        for p, piece in enumerate(pieces):
            rows, depth = piece.shape
            row = pl.multiple_of(offsets[p // parts % sites], rows)
            column = offsets[sites + p % parts] + p // (sites * parts) * depth
            put(split_ref, piece[...], row, pl.multiple_of(column, depth))

    products(split_ref, c_ref, add[0] if add else None, o_ref, share)


def whole_kernel(added, block_ref, c_ref, *refs):
    o_ref, split_ref = refs[-2:]
    k, depth = pl.program_id(1), c_ref.shape[0]

    @pl.when(pl.program_id(0) == 0)
    def _():
        for j in range(block_ref.shape[0]):
            put(split_ref, block_ref[j, 0], j * block_ref.shape[2], pl.multiple_of(k * depth, depth))

    products(split_ref, c_ref, refs[0] if added else None, o_ref, (0, 1))


def step_kernel(tiles, arrived, x_ref, y_ref, own_ref, *refs):
    x_out_ref, y_out_ref = refs[-2:]
    chunk = pl.program_id(0) // tiles
    for c in range((len(refs) - 2) // arrived):

        @pl.when(chunk == c)
        def _():
            coupled = own_ref[...]
            for term in refs[c * arrived : (c + 1) * arrived]:
                coupled += term[...]
            x, y = x_ref[...], y_ref[...]
            radius = x * x + y * y
            y_next = y + time_step * (
                -(kerr_rate * radius - pump_rate + detuning) * x + coupling_gain * coupled
            )
            radius_next = x * x + y_next * y_next
            x_out_ref[...] = x + time_step * (kerr_rate * radius_next + pump_rate + detuning) * y_next
            y_out_ref[...] = y_next


def oscillate(own, arrived, positions, momenta):
    rows, width = positions.shape
    chunk = width // len(arrived)
    tile = tile_of(chunk)
    tiles = chunk // tile
    there = pl.BlockSpec((rows, tile), lambda i: (0, i))
    here = [
        pl.BlockSpec((rows, tile), lambda i, c=c: (0, jnp.clip(i - c * tiles, 0, tiles - 1)))
        for c, terms in enumerate(arrived)
        for _ in terms
    ]
    return pl.pallas_call(
        functools.partial(step_kernel, tiles, len(arrived[0])),
        grid=(width // tile,),
        in_specs=[there] * 3 + here,
        out_specs=[there, there],
        out_shape=[jax.ShapeDtypeStruct(positions.shape, f32)] * 2,
        compiler_params=pltpu.CompilerParams(vmem_limit_bytes=VMEM),
        name="oscillate",
    )(positions, momenta, own, *[term for terms in arrived for term in terms])


def tile_of(width):
    return max(t for t in range(128, 513, 128) if width % t == 0)


def shard_product(shard, couplings, lanes, parts, rows, add=None, offsets=None, share=(0, 1)):
    h, of = share
    start, width = lanes.start, lanes.stop - lanes.start
    depth = couplings.shape[0] // (parts * of)
    tile = tile_of(width)
    result = pl.BlockSpec((rows, tile), lambda i, k, *_: (0, i))
    couple = pl.BlockSpec((depth, tile), lambda i, k, *_: (k * of + h, start // tile + i))
    if offsets is not None:
        values, scalars = list(shard), [offsets]
        sites = offsets.shape[0] - parts
        kernel = functools.partial(pieces_kernel, sites, parts, share, int(add is not None))
        in_specs = [
            pl.BlockSpec(x.shape, lambda i, k, *_: (0, 0), pipeline_mode=pl.Buffered(1)) for x in values
        ]
    else:
        values, scalars = [shard], []
        kernel = functools.partial(whole_kernel, add is not None)
        block = (shard.shape[0], 1, *shard.shape[2:])
        in_specs = [pl.BlockSpec(block, lambda i, k, *_: (0, jnp.where(i == 0, k, parts - 1), 0, 0))]
    return pl.pallas_call(
        kernel,
        grid_spec=pltpu.PrefetchScalarGridSpec(
            num_scalar_prefetch=len(scalars),
            grid=(width // tile, parts),
            in_specs=in_specs + [couple] + ([] if add is None else [result]),
            out_specs=result,
            scratch_shapes=[pltpu.VMEM((2, rows, couplings.shape[0]), bf16)],
        ),
        out_shape=jax.ShapeDtypeStruct((rows, width), f32),
        compiler_params=pltpu.CompilerParams(vmem_limit_bytes=VMEM),
        cost_estimate=pl.CostEstimate(
            flops=WORK * rows * width * depth * parts, bytes_accessed=0, transcendentals=0
        ),
        name="products",
    )(*scalars, *values, couplings, *([] if add is None else [add]))


def after(x, *others):
    return lax.optimization_barrier((x, *others))[0]


class Plan:
    def __init__(self, n, cols):
        self.n, self.cols, self.ratio = n, cols, cols // n
        assert self.ratio * n == cols
        self.order = [[self.shift(z, a) for a in range(n - 1, -1, -1)] for z in range(n)]
        self.slot = [[self.order[z].index(s) for s in range(n)] for z in range(n)]

    def shift(self, a, b):
        return a ^ b if self.n & (self.n - 1) == 0 else (a + b) % self.n

    def unshift(self, a, b):
        return a ^ b if self.n & (self.n - 1) == 0 else (a - b) % self.n

    def messages(self, t, k):
        n, rounds = self.n, []
        for z in range(t + 1):
            if z < n - 1 and self.slot[z][n - 1 - t + z] == k:
                pair = [(z, z + 1), (n - 1 - z, n - 2 - z)]
                for others in rounds:
                    both = others + pair
                    if len({a for a, _ in both}) == len({b for _, b in both}) == len(both):
                        others += pair
                        break
                else:
                    rounds.append(pair)
        return rounds

    def sources(self, t, k):
        n, out = self.n, {}
        for pairs in self.messages(t, k):
            out.update((a, 2 * a - b if 0 <= 2 * a - b < n else None) for a, b in pairs)
        if k == t:
            for later in range(t + 1, n - 1):
                for pairs in self.messages(later, k):
                    out.update((a, None) for a, _ in pairs)
        return out

    def site_pairs(self, m):
        r = self.ratio
        return [(q * r + c, self.shift(q, m) * r + c) for q in range(self.n) for c in range(r)]


def shift(plan, a, b):
    return a ^ b if plan.n & (plan.n - 1) == 0 else lax.rem(a + b, plan.n)


def unshift(plan, a, b):
    return a ^ b if plan.n & (plan.n - 1) == 0 else lax.rem(a - b + plan.n, plan.n)


def one_of(values, index):
    out = values[0]
    for i in range(1, len(values)):
        out = jnp.where(index == i, values[i], out)
    return out


def pick(values, choice, index):
    used = sorted({c for c in choice if c is not None})
    out = values[used[0]]
    for c in used[1:]:
        mine = functools.reduce(jnp.logical_or, [index == i for i, v in enumerate(choice) if v == c])
        out = jnp.where(mine, values[c], out)
    return out


def spread_sites(plan, positions, col, start, depth):
    n = plan.n
    site = col // plan.ratio
    rows = positions.shape[0] // n
    arrived = []
    for m in range(n):
        part = lax.dynamic_slice(positions, (shift(plan, site, m) * rows, start), (rows, depth))
        arrived.append(part if m == 0 else lax.ppermute(part, "col", plan.site_pairs(m)))
    return arrived


def exchange_rows(plan, k, arrived, row, col, *before):
    n = plan.n
    target = [[plan.order[z][k] for z in range(n)].index(r) for r in range(n)]
    part = one_of(arrived, unshift(plan, col // plan.ratio, one_of(target, row)))
    if before:
        part = after(part, *before)
    pairs = [(r, target[r]) for r in range(n)]
    return lax.ppermute(part, "row", pairs) if any(a != b for a, b in pairs) else part


def gather_plane(plan, part):
    whole = lax.all_gather(part, "col", axis=0, tiled=False)
    return whole.reshape(plan.n, plan.ratio, *part.shape)


def gather_sites(plan, part):
    return [part if m == 0 else lax.ppermute(part, "col", plan.site_pairs(m)) for m in range(plan.n)]


def gather_parts(plan, pieces):
    r = plan.ratio
    turns = [[(q * r + c, q * r + (c + d) % r) for q in range(plan.n) for c in range(r)] for d in range(r)]
    return [p if d == 0 else lax.ppermute(p, "col", turns[d]) for p in pieces for d in range(r)]


def piece_offsets(plan, rows, depth, start, col):
    n, r = plan.n, plan.ratio
    site, part = col // r, lax.rem(col, r)
    starts = [unshift(plan, site, m) * rows for m in range(n)]
    starts += [lax.rem(part - d + r, r) * depth + start for d in range(r)]
    return jnp.stack(starts).astype(jnp.int32)


class Sums:
    def __init__(self):
        self.arrays = []

    def add(self, array, pairs):
        self.arrays.append((array, {b: a for a, b in pairs}))

    def carried(self, wanted, row):
        def serves(heard, z):
            return heard.get(z) == wanted[z]

        for array, heard in self.arrays:
            if all(serves(heard, z) for z in wanted):
                return array
        out = None
        for array, heard in self.arrays:
            mine = functools.reduce(
                jnp.logical_or, [row == z for z in wanted if wanted[z] is not None and serves(heard, z)], False
            )
            kept = jnp.where(mine, array, 0.0)
            out = kept if out is None else out + kept
        return out


def per_device(plan, positions, momenta, couplings):
    n = plan.n
    row, col = lax.axis_index("row"), lax.axis_index("col")
    width = positions.shape[1]
    chunk = width // CHUNKS
    lanes = [slice(c * chunk, (c + 1) * chunk) for c in range(CHUNKS)]

    depth = width // SHARES
    spread = [spread_sites(plan, positions, col, h * depth, depth) for h in range(SHARES)]
    own = []
    for h in range(SHARES):
        own.append(exchange_rows(plan, 0, spread[h], row, col, *own[-1:]))
    opening = [gather_sites(plan, part) for part in own]
    second = []
    for h in range(SHARES):
        second.append(exchange_rows(plan, 1, spread[h], row, col, own[-1]))
    spread = [jnp.concatenate(share, axis=1) for share in zip(*spread)]
    shares = [None, second[-1]]
    for k in range(2, n):
        before = own[-1:] if k < n - 1 else [shares[-1]]
        shares.append(exchange_rows(plan, k, spread, row, col, *before))

    partial = [[None] * CHUNKS for _ in range(n)]
    sums = [[Sums() for _ in range(CHUNKS)] for _ in range(n)]
    rows = positions.shape[0]
    first, pieces = None, []
    for h in range(SHARES):
        part = opening[h]
        if h:
            couplings = after(couplings, first, shares[2], *second[:-1])
            part = [after(piece, first) for piece in part]
        part = gather_parts(plan, part)
        pieces += part
        first = shard_product(
            part,
            couplings,
            lanes[0],
            plan.ratio,
            rows,
            add=first,
            offsets=piece_offsets(plan, rows // n, width, h * depth, col),
            share=(h, SHARES),
        )
    partial[0][0] = last = first
    shares[1] = jnp.concatenate([after(part, first) for part in second], axis=1)
    shards = [pieces] + [gather_plane(plan, after(part, first, shares[-2])) for part in shares[1:]]
    couplings = after(couplings, *shares[1:])
    for t in range(n):
        for c, span in enumerate(lanes if t < n - 1 else [slice(0, width)]):
            add = None
            if 0 < t < n - 1:
                add = sums[t - 1][c].carried(plan.sources(t, t), row)
            if t or c:
                before = [array for array, _ in sums[t - 1][c].arrays] if 0 < t < n - 1 else []
                couplings = after(couplings, last, *sent, *before)
                offsets = None if t else piece_offsets(plan, rows // n, width, 0, col)
                last = shard_product(shards[t], couplings, span, plan.ratio, rows, add=add, offsets=offsets)
                partial[t][c] = last
            sent = []
            for k in range(t + 1):
                mine = partial[t][c]
                if k < t:
                    if not plan.messages(t, k):
                        continue
                    mine = after(partial[k][c], partial[t][c]) + sums[t - 1][c].carried(plan.sources(t, k), row)
                sent.append(mine)
                for pairs in plan.messages(t, k):
                    sums[t][c].add(lax.ppermute(mine, "row", pairs), pairs)
    arrived = [[array for array, _ in sums[n - 2][c].arrays] for c in range(CHUNKS)]
    return oscillate(last, arrived, positions, momenta)


def solution(mesh):
    placed = (P("row", "col"), P("row", "col"), P("row", "col"))
    plan = Plan(mesh.shape["row"], mesh.shape["col"])

    def step(positions, momenta, couplings):
        return per_device(plan, positions, momenta, couplings)

    return jax.shard_map(
        step,
        mesh=mesh,
        in_specs=placed,
        out_specs=(P("row", "col"), P("row", "col")),
        check_vma=False,
    )
```

```python
import functools

import jax
import jax.numpy as jnp
from jax import lax
from jax.experimental import pallas as pl
from jax.experimental.pallas import tpu as pltpu
from jax.sharding import PartitionSpec as P

time_step = 0.5
kerr_rate = 1.0
pump_rate = 0.6
detuning = 0.4
coupling_gain = 1.5

CHUNKS = 2
SHARES = 2
WORK = 0
VMEM = 60 * 2**20
f32, bf16 = jnp.float32, jnp.bfloat16


def halves(x):
    high = x.astype(bf16)
    return high, (x - high.astype(f32)).astype(bf16)


def products(split_ref, c_ref, add_ref, o_ref, share):
    k, (h, of), depth = pl.program_id(1), share, c_ref.shape[0]
    columns = pl.ds(pl.multiple_of((k * of + h) * depth, depth), depth)
    high, low = halves(c_ref[...])
    p_high = split_ref[0, :, columns]
    part = jnp.dot(p_high, high, preferred_element_type=f32)
    part += jnp.dot(split_ref[1, :, columns], high, preferred_element_type=f32)
    part += jnp.dot(p_high, low, preferred_element_type=f32)

    @pl.when(k == 0)
    def _():
        o_ref[...] = part if add_ref is None else add_ref[...] + part

    @pl.when(k > 0)
    def _():
        o_ref[...] += part


def put(split_ref, piece, row, column):
    rows, columns = pl.ds(row, piece.shape[0]), pl.ds(column, piece.shape[1])
    split_ref[0, rows, columns], split_ref[1, rows, columns] = halves(piece)


def pieces_kernel(sites, parts, share, added, offsets, *refs):
    (c_ref, *add), (o_ref, split_ref) = refs[-3 - added : -2], refs[-2:]
    pieces = refs[: -3 - added]

    @pl.when((pl.program_id(0) == 0) & (pl.program_id(1) == 0))
    def _():
        for p, piece in enumerate(pieces):
            rows, depth = piece.shape
            row = pl.multiple_of(offsets[p // parts % sites], rows)
            column = offsets[sites + p % parts] + (share[0] + p // (sites * parts)) * depth
            put(split_ref, piece[...], row, pl.multiple_of(column, depth))

    products(split_ref, c_ref, add[0] if add else None, o_ref, share)


def whole_kernel(added, block_ref, c_ref, *refs):
    o_ref, split_ref = refs[-2:]
    k, depth = pl.program_id(1), c_ref.shape[0]

    @pl.when(pl.program_id(0) == 0)
    def _():
        for j in range(block_ref.shape[0]):
            put(split_ref, block_ref[j, 0], j * block_ref.shape[2], pl.multiple_of(k * depth, depth))

    products(split_ref, c_ref, refs[0] if added else None, o_ref, (0, 1))


def step_kernel(tiles, arrived, x_ref, y_ref, own_ref, *refs):
    x_out_ref, y_out_ref = refs[-2:]
    chunk = pl.program_id(0) // tiles
    for c in range((len(refs) - 2) // arrived):

        @pl.when(chunk == c)
        def _():
            coupled = own_ref[...]
            for term in refs[c * arrived : (c + 1) * arrived]:
                coupled += term[...]
            x, y = x_ref[...], y_ref[...]
            radius = x * x + y * y
            y_next = y + time_step * (
                -(kerr_rate * radius - pump_rate + detuning) * x + coupling_gain * coupled
            )
            radius_next = x * x + y_next * y_next
            x_out_ref[...] = x + time_step * (kerr_rate * radius_next + pump_rate + detuning) * y_next
            y_out_ref[...] = y_next


def oscillate(own, arrived, positions, momenta):
    rows, width = positions.shape
    chunk = width // len(arrived)
    tile = tile_of(chunk, 256)
    tiles = chunk // tile
    there = pl.BlockSpec((rows, tile), lambda i: (0, i))
    here = [
        pl.BlockSpec((rows, tile), lambda i, c=c: (0, jnp.clip(i - c * tiles, 0, tiles - 1)))
        for c, terms in enumerate(arrived)
        for _ in terms
    ]
    return pl.pallas_call(
        functools.partial(step_kernel, tiles, len(arrived[0])),
        grid=(width // tile,),
        in_specs=[there] * 3 + here,
        out_specs=[there, there],
        out_shape=[jax.ShapeDtypeStruct(positions.shape, f32)] * 2,
        compiler_params=pltpu.CompilerParams(vmem_limit_bytes=VMEM),
        name="oscillate",
    )(positions, momenta, own, *[term for terms in arrived for term in terms])


def tile_of(width, most=512):
    return max(t for t in range(128, most + 1, 128) if width % t == 0)


def shard_product(shard, couplings, lanes, parts, rows, add=None, offsets=None, share=(0, 1)):
    h, of = share
    start, width = lanes.start, lanes.stop - lanes.start
    depth = couplings.shape[0] // (parts * of)
    tile = tile_of(width)
    result = pl.BlockSpec((rows, tile), lambda i, k, *_: (0, i))
    couple = pl.BlockSpec((depth, tile), lambda i, k, *_: (k * of + h, start // tile + i))
    if offsets is not None:
        values, scalars = list(shard), [offsets]
        sites = offsets.shape[0] - parts
        kernel = functools.partial(pieces_kernel, sites, parts, share, int(add is not None))
        in_specs = [
            pl.BlockSpec(x.shape, lambda i, k, *_: (0, 0), pipeline_mode=pl.Buffered(1)) for x in values
        ]
    else:
        values, scalars = [shard], []
        kernel = functools.partial(whole_kernel, add is not None)
        block = (shard.shape[0], 1, *shard.shape[2:])
        in_specs = [pl.BlockSpec(block, lambda i, k, *_: (0, jnp.where(i == 0, k, parts - 1), 0, 0))]
    return pl.pallas_call(
        kernel,
        grid_spec=pltpu.PrefetchScalarGridSpec(
            num_scalar_prefetch=len(scalars),
            grid=(width // tile, parts),
            in_specs=in_specs + [couple] + ([] if add is None else [result]),
            out_specs=result,
            scratch_shapes=[pltpu.VMEM((2, rows, couplings.shape[0]), bf16)],
        ),
        out_shape=jax.ShapeDtypeStruct((rows, width), f32),
        compiler_params=pltpu.CompilerParams(vmem_limit_bytes=VMEM),
        cost_estimate=pl.CostEstimate(
            flops=WORK * rows * width * depth * parts, bytes_accessed=0, transcendentals=0
        ),
        name="products",
    )(*scalars, *values, couplings, *([] if add is None else [add]))


def after(x, *others):
    return lax.optimization_barrier((x, *others))[0]


class Plan:
    def __init__(self, n, cols):
        self.n, self.cols, self.ratio = n, cols, cols // n
        assert self.ratio * n == cols
        self.order = [[self.shift(z, a) for a in range(n - 1, -1, -1)] for z in range(n)]
        self.slot = [[self.order[z].index(s) for s in range(n)] for z in range(n)]

    def shift(self, a, b):
        return a ^ b if self.n & (self.n - 1) == 0 else (a + b) % self.n

    def unshift(self, a, b):
        return a ^ b if self.n & (self.n - 1) == 0 else (a - b) % self.n

    def messages(self, t, k):
        n, rounds = self.n, []
        for z in range(t + 1):
            if z < n - 1 and self.slot[z][n - 1 - t + z] == k:
                pair = [(z, z + 1), (n - 1 - z, n - 2 - z)]
                for others in rounds:
                    both = others + pair
                    if len({a for a, _ in both}) == len({b for _, b in both}) == len(both):
                        others += pair
                        break
                else:
                    rounds.append(pair)
        return rounds

    def sources(self, t, k):
        n, out = self.n, {}
        for pairs in self.messages(t, k):
            out.update((a, 2 * a - b if 0 <= 2 * a - b < n else None) for a, b in pairs)
        if k == t:
            for later in range(t + 1, n - 1):
                for pairs in self.messages(later, k):
                    out.update((a, None) for a, _ in pairs)
        return out

    def site_pairs(self, m):
        r = self.ratio
        return [(q * r + c, self.shift(q, m) * r + c) for q in range(self.n) for c in range(r)]


def shift(plan, a, b):
    return a ^ b if plan.n & (plan.n - 1) == 0 else lax.rem(a + b, plan.n)


def unshift(plan, a, b):
    return a ^ b if plan.n & (plan.n - 1) == 0 else lax.rem(a - b + plan.n, plan.n)


def one_of(values, index):
    out = values[0]
    for i in range(1, len(values)):
        out = jnp.where(index == i, values[i], out)
    return out


def pick(values, choice, index):
    used = sorted({c for c in choice if c is not None})
    out = values[used[0]]
    for c in used[1:]:
        mine = functools.reduce(jnp.logical_or, [index == i for i, v in enumerate(choice) if v == c])
        out = jnp.where(mine, values[c], out)
    return out


def spread_sites(plan, positions, col, start, depth):
    n = plan.n
    site = col // plan.ratio
    rows = positions.shape[0] // n
    arrived = []
    for m in range(n):
        part = lax.dynamic_slice(positions, (shift(plan, site, m) * rows, start), (rows, depth))
        arrived.append(part if m == 0 else lax.ppermute(part, "col", plan.site_pairs(m)))
    return arrived


def exchange_rows(plan, k, arrived, row, col, *before):
    n = plan.n
    target = [[plan.order[z][k] for z in range(n)].index(r) for r in range(n)]
    part = one_of(arrived, unshift(plan, col // plan.ratio, one_of(target, row)))
    if before:
        part = after(part, *before)
    pairs = [(r, target[r]) for r in range(n)]
    return lax.ppermute(part, "row", pairs) if any(a != b for a, b in pairs) else part


def gather_plane(plan, part):
    whole = lax.all_gather(part, "col", axis=0, tiled=False)
    return whole.reshape(plan.n, plan.ratio, *part.shape)


def gather_sites(plan, part):
    return [part if m == 0 else lax.ppermute(part, "col", plan.site_pairs(m)) for m in range(plan.n)]


def gather_parts(plan, pieces):
    r = plan.ratio
    turns = [[(q * r + c, q * r + (c + d) % r) for q in range(plan.n) for c in range(r)] for d in range(r)]
    return [p if d == 0 else lax.ppermute(p, "col", turns[d]) for p in pieces for d in range(r)]


def piece_offsets(plan, rows, depth, col):
    n, r = plan.n, plan.ratio
    site, part = col // r, lax.rem(col, r)
    starts = [unshift(plan, site, m) * rows for m in range(n)]
    starts += [lax.rem(part - d + r, r) * depth for d in range(r)]
    return jnp.stack(starts).astype(jnp.int32)


class Sums:
    def __init__(self):
        self.arrays = []

    def add(self, array, pairs):
        self.arrays.append((array, {b: a for a, b in pairs}))

    def carried(self, wanted, row):
        def serves(heard, z):
            return heard.get(z) == wanted[z]

        for array, heard in self.arrays:
            if all(serves(heard, z) for z in wanted):
                return array
        out = None
        for array, heard in self.arrays:
            mine = functools.reduce(
                jnp.logical_or, [row == z for z in wanted if wanted[z] is not None and serves(heard, z)], False
            )
            kept = jnp.where(mine, array, 0.0)
            out = kept if out is None else out + kept
        return out


def per_device(plan, positions, momenta, couplings):
    n = plan.n
    row, col = lax.axis_index("row"), lax.axis_index("col")
    width = positions.shape[1]
    chunk = width // CHUNKS
    lanes = [slice(c * chunk, (c + 1) * chunk) for c in range(CHUNKS)]

    depth = width // SHARES
    spread = [spread_sites(plan, positions, col, h * depth, depth) for h in range(SHARES)]
    own = []
    for h in range(SHARES):
        own.append(exchange_rows(plan, 0, spread[h], row, col, *own[-1:]))
    opening = [gather_sites(plan, part) for part in own]
    second = []
    for h in range(SHARES):
        second.append(exchange_rows(plan, 1, spread[h], row, col, own[-1]))
    spread = [jnp.concatenate(share, axis=1) for share in zip(*spread)]
    shares = [None, second[-1]]
    for k in range(2, n):
        before = own[-1:] if k < n - 1 else [shares[-1]]
        shares.append(exchange_rows(plan, k, spread, row, col, *before))

    partial = [[None] * CHUNKS for _ in range(n)]
    sums = [[Sums() for _ in range(CHUNKS)] for _ in range(n)]
    rows = positions.shape[0]
    first, pieces, offsets = None, [], piece_offsets(plan, rows // n, width, col)
    for h in range(SHARES):
        part = opening[h]
        if h:
            couplings = after(couplings, first, shares[2], *second[:-1])
            part = [after(piece, first) for piece in part]
        part = gather_parts(plan, part)
        pieces += part
        first = shard_product(
            part,
            couplings,
            lanes[0],
            plan.ratio,
            rows,
            add=first,
            offsets=offsets,
            share=(h, SHARES),
        )
    partial[0][0] = last = first
    shares[1] = jnp.concatenate([after(part, first) for part in second], axis=1)
    shards = [pieces] + [gather_plane(plan, after(part, first, shares[-2])) for part in shares[1:]]
    couplings = after(couplings, *shares[1:])
    for t in range(n):
        for c, span in enumerate(lanes if t < n - 1 else [slice(0, width)]):
            add = None
            if 0 < t < n - 1:
                add = sums[t - 1][c].carried(plan.sources(t, t), row)
            if t or c:
                before = [array for array, _ in sums[t - 1][c].arrays] if 0 < t < n - 1 else []
                couplings = after(couplings, last, *sent, *before)
                last = shard_product(shards[t], couplings, span, plan.ratio, rows, add, None if t else offsets)
                partial[t][c] = last
            sent = []
            for k in range(t + 1):
                mine = partial[t][c]
                if k < t:
                    if not plan.messages(t, k):
                        continue
                    mine = after(partial[k][c], partial[t][c]) + sums[t - 1][c].carried(plan.sources(t, k), row)
                sent.append(mine)
                for pairs in plan.messages(t, k):
                    sums[t][c].add(lax.ppermute(mine, "row", pairs), pairs)
    arrived = [[array for array, _ in sums[n - 2][c].arrays] for c in range(CHUNKS)]
    return oscillate(last, arrived, positions, momenta)


def solution(mesh):
    placed = (P("row", "col"), P("row", "col"), P("row", "col"))
    plan = Plan(mesh.shape["row"], mesh.shape["col"])

    def step(positions, momenta, couplings):
        return per_device(plan, positions, momenta, couplings)

    return jax.shard_map(
        step,
        mesh=mesh,
        in_specs=placed,
        out_specs=(P("row", "col"), P("row", "col")),
        check_vma=False,
    )
```
